128 devices in a mesh: rep: 32 (over y, z, core), shard: 4 (over x).
Axes of the slice: x: 4, y: 4, z: 4, core: 2. Of those that a mesh axis runs over, the one named last changes fastest.
Arguments:
- grads: bfloat16 [32, 16777216], P('rep', 'shard'), may hold values from -64 to 64
Outputs:
- aggregate: bfloat16 [16777216], P('shard')
- weights: float32 [32], replicated
The draws below stay inside these ranges and needn't reach their ends.
All inputs are finite; a program needn't handle non-finite values.
Results may differ from the reference program's by a relative error of at most 0.0034.
Values may be sent and summed in bfloat16 or wider, within the bound.
No kernel may reach another device: no remote copies, remote signals or barrier semaphores. Data moves between devices by JAX's collectives and lax.ppermute only.
A program may use at most 128 MiB of HBM per device.

```python
import math
import jax
import jax.numpy as jnp
from jax import lax

ITERS = 4
REPLICAS = 32
COORDS = 16777216


def draw_grads(key, part):
    key = jax.random.fold_in(key, 7)
    first, second, third, fourth, fifth, sixth, seventh = jax.random.split(key, 7)
    common = jax.random.truncated_normal(first, -5.0, 5.0, (COORDS,), jnp.float32)
    noise = jax.random.truncated_normal(second, -5.0, 5.0, (REPLICAS, COORDS), jnp.float32)
    lowest = 0.6
    rising = 1.0 + 2.0 * jnp.arange(COORDS, dtype=jnp.float32) / COORDS
    rough = jnp.exp(jax.random.uniform(fourth, (COORDS,), jnp.float32, -0.3, 0.3))
    segments = 4 * REPLICAS
    seg_length = max(1, COORDS // segments)
    position = jnp.arange(COORDS, dtype=jnp.int32)
    segment = jnp.minimum(position // seg_length, segments - 1)
    factor = jnp.exp(jax.random.uniform(seventh, (REPLICAS, segments), jnp.float32, math.log(0.2), math.log(8.0)))
    local_scale = jnp.take(factor, segment, axis=1)
    spike_scale = jnp.exp(jax.random.uniform(third, (REPLICAS, 1), jnp.float32, math.log(5.0), math.log(45.0)))
    signed = jax.random.uniform(fifth, (REPLICAS, COORDS), jnp.float32, -1.0, 1.0)
    magnitude = lowest + (1.0 - lowest) * jnp.abs(signed)
    direction = jnp.where(signed > 0.0, 1.0, -1.0)
    rate = 1.0 / min(32768, max(8, COORDS // 512))
    placed = jax.random.bernoulli(sixth, rate, (REPLICAS, COORDS))
    spikes = jnp.where(placed, direction * magnitude * spike_scale, 0.0)
    values = 0.5 * common * (rising * rough) + 0.06 * noise * rising * local_scale + spikes
    return values.astype(jnp.bfloat16)


def setup_inputs(seed: int = 0) -> dict:
    keys = jax.random.split(jax.random.key(seed), 2)
    return {
        "grads": draw_grads(jax.random.fold_in(keys[1], 71), 0),
    }


def weiszfeld(gram, total):
    count = gram.shape[0]
    diag = jnp.diagonal(gram)
    weights = jnp.full((count,), 1.0 / count, dtype=jnp.float32)
    for step in range(ITERS):
        query = jnp.dot(gram, weights, precision=lax.Precision.HIGHEST)
        spread = jnp.dot(weights, query, precision=lax.Precision.HIGHEST)
        square = jnp.maximum((diag - 2.0 * query + spread) / total, 0.0)
        inverse = 1.0 / jnp.sqrt(square + 1e-06)
        weights = inverse / jnp.sum(inverse)
    return weights

def reference(grads):
    gram = lax.dot_general(grads, grads, (((1,), (1,)), ((), ())), preferred_element_type=jnp.float32)
    weights = weiszfeld(gram, COORDS)
    coeffs = weights.astype(jnp.bfloat16)
    aggregate = jnp.dot(coeffs, grads, preferred_element_type=jnp.float32).astype(jnp.bfloat16)
    return (aggregate, weights)
```

```python
import functools

import jax
import jax.numpy as jnp
from jax import lax
from jax.experimental import pallas as pl
from jax.experimental.pallas import tpu as pltpu
from jax.sharding import PartitionSpec as P

ITERS = 4
LANES = 128
PACK = 16
VMEM = 48 * 1024 * 1024


def compact_kernel(x_ref, o_ref):
    o_ref[...] = x_ref[...].reshape(o_ref.shape)


def compact(grads, steps):
    size = grads.shape[1]
    rows = size // LANES
    return pl.pallas_call(
        compact_kernel,
        grid=(steps,),
        in_specs=[pl.BlockSpec((1, size // steps), lambda i: (0, i))],
        out_specs=pl.BlockSpec((rows // steps, LANES), lambda i: (i, 0)),
        out_shape=jax.ShapeDtypeStruct((rows, LANES), grads.dtype),
        compiler_params=pltpu.CompilerParams(vmem_limit_bytes=VMEM),
        cost_estimate=pl.CostEstimate(flops=0, bytes_accessed=6 * size, transcendentals=0),
    )(grads)


def gram_kernel(steps, x_ref, o_ref, total):
    step = pl.program_id(0)
    count, rows, _ = x_ref.shape
    wide = count * PACK
    left = jnp.concatenate(
        [x_ref[:, j * PACK : (j + 1) * PACK, :].reshape(wide, LANES) for j in range(rows // PACK)], axis=1
    )
    product = lax.dot_general(left, left, (((1,), (1,)), ((), ())), preferred_element_type=jnp.float32)

    @pl.when(step == 0)
    def _():
        total[...] = product

    @pl.when(step > 0)
    def _():
        total[...] += product

    @pl.when(step == steps - 1)
    def _():
        i = lax.broadcasted_iota(jnp.int32, (wide, wide), 0)
        j = lax.broadcasted_iota(jnp.int32, (wide, wide), 1)
        kept = jnp.where(i % PACK == j % PACK, total[...], 0.0)
        folded = kept.reshape(count, PACK, wide).sum(axis=1)
        k = lax.broadcasted_iota(jnp.int32, (wide, LANES), 0)
        s = lax.broadcasted_iota(jnp.int32, (wide, LANES), 1)
        fold = jnp.where(k // PACK == s % count, 1.0, 0.0)
        spread = jnp.dot(folded, fold, precision=lax.Precision.HIGHEST, preferred_element_type=jnp.float32)
        r = lax.broadcasted_iota(jnp.int32, (count, LANES), 0)
        t = lax.broadcasted_iota(jnp.int32, (count, LANES), 1)
        kept = jnp.where(t // count == r // 8, spread, 0.0)
        o_ref[...] = kept.reshape(count // 8, 8, LANES).sum(axis=0)


def partial_gram(blocks, steps):
    count, rows, _ = blocks.shape
    wide = count * PACK
    return pl.pallas_call(
        functools.partial(gram_kernel, steps),
        grid=(steps,),
        in_specs=[pl.BlockSpec((count, rows // steps, LANES), lambda i: (0, i, 0))],
        out_specs=pl.BlockSpec((8, LANES), lambda i: (0, 0)),
        out_shape=jax.ShapeDtypeStruct((8, LANES), jnp.float32),
        scratch_shapes=[pltpu.VMEM((wide, wide), jnp.float32)],
        compiler_params=pltpu.CompilerParams(vmem_limit_bytes=VMEM),
    )(blocks)


def aggregate_kernel(total, g_ref, x_ref, o_ref, w_ref, coeffs):
    count = x_ref.shape[0]

    @pl.when(pl.program_id(0) == 0)
    def _():
        gram = g_ref[...].sum(axis=0)
        gram = jnp.concatenate([gram] * (count // 8), axis=0)
        r = lax.broadcasted_iota(jnp.int32, (count, LANES), 0)
        t = lax.broadcasted_iota(jnp.int32, (count, LANES), 1)
        gram = jnp.where(t // count == r // 8, gram, 0.0)
        same = (t % count == r).astype(jnp.float32)
        diag = jnp.sum(gram * same, axis=1, keepdims=True)
        weights = jnp.full((count, 1), 1.0 / count, jnp.float32)
        for _ in range(ITERS):
            across = jnp.sum(same * weights, axis=0, keepdims=True)
            query = jnp.sum(gram * across, axis=1, keepdims=True)
            spread = jnp.sum(weights * query, axis=0, keepdims=True)
            square = jnp.maximum((diag - 2.0 * query + spread) / total, 0.0)
            inverse = 1.0 / jnp.sqrt(square + 1e-06)
            weights = inverse / jnp.sum(inverse, axis=0, keepdims=True)
        w_ref[...] = jnp.sum(same * weights, axis=0, keepdims=True)
        coeffs[...] = jnp.broadcast_to(weights.astype(jnp.bfloat16).astype(jnp.float32), (count, LANES))

    rows = x_ref.shape[1]
    piece = 32
    for k in range(rows // piece):
        at = slice(k * piece, (k + 1) * piece)
        parts = [None] * 4
        for r in range(count):
            term = x_ref[r, at, :].astype(jnp.float32) * coeffs[r : r + 1, :]
            parts[r % 4] = term if parts[r % 4] is None else parts[r % 4] + term
        o_ref[at, :] = ((parts[0] + parts[1]) + (parts[2] + parts[3])).astype(o_ref.dtype)


def aggregate_blocks(grams, blocks, total, steps):
    count, rows, _ = blocks.shape
    return pl.pallas_call(
        functools.partial(aggregate_kernel, float(total)),
        grid=(steps,),
        in_specs=[
            pl.BlockSpec(grams.shape, lambda i: (0, 0, 0)),
            pl.BlockSpec((count, rows // steps, LANES), lambda i: (0, i, 0)),
        ],
        out_specs=[
            pl.BlockSpec((rows // steps, LANES), lambda i: (i, 0)),
            pl.BlockSpec((1, LANES), lambda i: (0, 0)),
        ],
        out_shape=[
            jax.ShapeDtypeStruct((rows, LANES), blocks.dtype),
            jax.ShapeDtypeStruct((1, LANES), jnp.float32),
        ],
        scratch_shapes=[pltpu.VMEM((count, LANES), jnp.float32)],
        compiler_params=pltpu.CompilerParams(vmem_limit_bytes=VMEM),
    )(grams, blocks)


def body(grads):
    count = lax.axis_size("rep")
    total = grads.shape[1] * lax.axis_size("shard")
    slab = compact(grads, 16).reshape(count, -1, LANES)
    blocks = lax.all_to_all(slab, "rep", split_axis=0, concat_axis=0, tiled=True)
    gram = partial_gram(blocks, 8)
    everyone = count * lax.axis_size("shard")
    grams = lax.all_to_all(
        jnp.broadcast_to(gram[None], (everyone, 8, LANES)), ("rep", "shard"), 0, 0, tiled=True
    )
    local, weights = aggregate_blocks(grams, blocks, total, 8)
    aggregate = lax.all_gather(local.reshape(-1), "rep", axis=0, tiled=True)
    return (aggregate, weights[0, :count])


def solution(mesh):
    placed = (P("rep", "shard"),)
    return jax.shard_map(
        body, mesh=mesh, in_specs=placed, out_specs=(P("shard"), P()), check_vma=False
    )
```

```python
import functools

import jax
import jax.numpy as jnp
from jax import lax
from jax.experimental import pallas as pl
from jax.experimental.pallas import tpu as pltpu
from jax.sharding import PartitionSpec as P

ITERS = 4
LANES = 128
PACK = 16
SIDE = 4
CORES = 2
COUNT = SIDE * SIDE * CORES
MIB = 1024 * 1024
ANY = pl.BlockSpec(memory_space=pl.ANY)


def compact_kernel(parts, piece, x_ref, o_ref, wide, packed, in_sems, out_sems):
    size = x_ref.shape[1] // parts
    rows = size // LANES
    loads, stores = [], []
    for i in range(parts):
        loads.append(
            pltpu.make_async_copy(x_ref.at[:, pl.ds(i * size, size)], wide.at[:, pl.ds(i * size, size)], in_sems.at[i])
        )
        stores.append(
            pltpu.make_async_copy(packed.at[pl.ds(i * rows, rows)], o_ref.at[pl.ds(i * rows, rows)], out_sems.at[i])
        )
        loads[i].start()
    for i in range(parts):
        loads[i].wait()

        @pl.loop(0, rows // piece)
        def _(j):
            at = pl.multiple_of(i * rows + j * piece, piece)
            values = wide[:, pl.ds(pl.multiple_of(at * LANES, piece * LANES), piece * LANES)]
            packed[pl.ds(at, piece), :] = values.reshape(piece, LANES)

        stores[i].start()
    for store in stores:
        store.wait()


def compact(grads, parts):
    size = grads.shape[1]
    rows = size // LANES
    return pl.pallas_call(
        functools.partial(compact_kernel, parts, 512),
        in_specs=[ANY],
        out_specs=ANY,
        out_shape=jax.ShapeDtypeStruct((rows, LANES), grads.dtype),
        scratch_shapes=[
            pltpu.VMEM((1, size), grads.dtype),
            pltpu.VMEM((rows, LANES), grads.dtype),
            pltpu.SemaphoreType.DMA((parts,)),
            pltpu.SemaphoreType.DMA((parts,)),
        ],
        compiler_params=pltpu.CompilerParams(vmem_limit_bytes=40 * MIB),
        cost_estimate=pl.CostEstimate(flops=0, bytes_accessed=6 * size, transcendentals=0),
    )(grads)


def load_rows(x_ref, held, sems, parts):
    rows = x_ref.shape[1] // parts
    loads = [
        pltpu.make_async_copy(
            x_ref.at[:, pl.ds(i * rows, rows), :], held.at[:, pl.ds(i * rows, rows), :], sems.at[i]
        )
        for i in range(parts)
    ]
    for load in loads:
        load.start()
    return loads


def fold(total):
    wide = total.shape[0]
    i = lax.broadcasted_iota(jnp.int32, (wide, wide), 0)
    j = lax.broadcasted_iota(jnp.int32, (wide, wide), 1)
    kept = jnp.where(i % PACK == j % PACK, total, 0.0)
    k = lax.broadcasted_iota(jnp.int32, (wide, LANES), 0)
    s = lax.broadcasted_iota(jnp.int32, (wide, LANES), 1)
    pick = jnp.where(k // PACK == s, 1.0, 0.0)
    columns = jnp.dot(kept, pick, precision=lax.Precision.HIGHEST, preferred_element_type=jnp.float32)
    return columns.reshape(wide // PACK, PACK, LANES).sum(axis=1)


def gram_kernel(parts, x_ref, o_ref, held, sems):
    loads = load_rows(x_ref, held, sems, parts)
    count, rows, _ = x_ref.shape
    half = count // 2
    rows = rows // parts
    product = functools.partial(
        lax.dot_general, dimension_numbers=(((1,), (1,)), ((), ())), preferred_element_type=jnp.float32
    )

    def group(first, part):
        return jnp.concatenate(
            [
                held[first : first + half, part * rows + j * PACK : part * rows + (j + 1) * PACK, :].reshape(
                    half * PACK, LANES
                )
                for j in range(rows // PACK)
            ],
            axis=1,
        )

    totals = None
    for part in range(parts):
        loads[part].wait()
        low, high = group(0, part), group(half, part)
        found = (product(low, low), product(high, low), product(high, high))
        totals = found if totals is None else tuple(a + b for a, b in zip(totals, found))
    low_low, high_low, high_high = (fold(t) for t in totals)
    square = jnp.concatenate([high_low, jnp.zeros((LANES - half, LANES), jnp.float32)], axis=0)
    low_high = square.T[:half]
    gram = jnp.concatenate(
        [low_low + pltpu.roll(low_high, half, 1), high_low + pltpu.roll(high_high, half, 1)], axis=0
    )
    for q in range(count // 8):
        part = gram[8 * q : 8 * (q + 1)]
        part = part if q == 0 else pltpu.roll(part, count * q, 1)
        o_ref[...] = part if q == 0 else o_ref[...] + part


def partial_gram(blocks, parts):
    return pl.pallas_call(
        functools.partial(gram_kernel, parts),
        in_specs=[ANY],
        out_shape=jax.ShapeDtypeStruct((8, LANES), jnp.float32),
        scratch_shapes=[pltpu.VMEM(blocks.shape, blocks.dtype), pltpu.SemaphoreType.DMA((parts,))],
        compiler_params=pltpu.CompilerParams(vmem_limit_bytes=32 * MIB),
    )(blocks)


def weiszfeld(grams, count, total):
    gram = grams.sum(axis=0)
    gram = jnp.concatenate([gram] * (count // 8), axis=0)
    r = lax.broadcasted_iota(jnp.int32, (count, LANES), 0)
    t = lax.broadcasted_iota(jnp.int32, (count, LANES), 1)
    gram = jnp.where(t // count == r // 8, gram, 0.0)
    same = (t % count == r).astype(jnp.float32)
    diag = jnp.sum(gram * same, axis=1, keepdims=True)
    weights = jnp.full((count, 1), 1.0 / count, jnp.float32)
    for _ in range(ITERS):
        across = jnp.sum(same * weights, axis=0, keepdims=True)
        query = jnp.sum(gram * across, axis=1, keepdims=True)
        spread = jnp.sum(weights * query, axis=0, keepdims=True)
        square = jnp.maximum((diag - 2.0 * query + spread) / total, 0.0)
        inverse = 1.0 / jnp.sqrt(square + 1e-06)
        weights = inverse / jnp.sum(inverse, axis=0, keepdims=True)
    return weights, same


def aggregate_kernel(total, parts, g_ref, x_ref, o_ref, w_ref, coeffs, held, sems):
    loads = load_rows(x_ref, held, sems, parts)
    count, rows, _ = x_ref.shape
    rows = rows // parts
    weights, same = weiszfeld(g_ref[...], count, total)
    w_ref[...] = jnp.sum(same * weights, axis=0, keepdims=True)
    coeffs[...] = jnp.broadcast_to(weights.astype(jnp.bfloat16).astype(jnp.float32), (count, LANES))
    piece = 32
    for part in range(parts):
        loads[part].wait()

        @pl.loop(0, rows // piece)
        def _(k):
            at = pl.ds(pl.multiple_of(part * rows + k * piece, piece), piece)
            sums = [None] * 4
            for r in range(count):
                term = held[r, at, :].astype(jnp.float32) * coeffs[r : r + 1, :]
                sums[r % 4] = term if sums[r % 4] is None else sums[r % 4] + term
            o_ref[at, :] = ((sums[0] + sums[1]) + (sums[2] + sums[3])).astype(o_ref.dtype)


def aggregate_blocks(grams, blocks, total, parts):
    count, rows, _ = blocks.shape
    return pl.pallas_call(
        functools.partial(aggregate_kernel, float(total), parts),
        in_specs=[pl.BlockSpec(memory_space=pltpu.VMEM), ANY],
        out_shape=[
            jax.ShapeDtypeStruct((rows, LANES), blocks.dtype),
            jax.ShapeDtypeStruct((1, LANES), jnp.float32),
        ],
        scratch_shapes=[
            pltpu.VMEM((count, LANES), jnp.float32),
            pltpu.VMEM(blocks.shape, blocks.dtype),
            pltpu.SemaphoreType.DMA((parts,)),
        ],
        compiler_params=pltpu.CompilerParams(vmem_limit_bytes=32 * MIB),
    )(grams, blocks)


def send(array, first, second):
    pairs = []
    for y in range(SIDE):
        for z in range(SIDE):
            for core in range(CORES):
                dy, dz = (first, second) if core == 0 else (second, first)
                there = (y + dy) % SIDE * SIDE + (z + dz) % SIDE
                pairs.append(((y * SIDE + z) * CORES + core, there * CORES + core))
    return lax.ppermute(array, "rep", pairs)


def swap(array):
    return lax.ppermute(array, "rep", [(i, i ^ 1) for i in range(COUNT)])


def place_kernel(moves, rows, *refs):
    sources, (out, held, in_sems, out_sems) = refs[: len(moves)], refs[-4:]
    me = lax.axis_index("rep")
    y, z, core = me // (SIDE * CORES), me // CORES % SIDE, me % CORES
    loads, stores = [], []
    for source, pieces in zip(sources, moves):
        for at, first, second, swapped in pieces:
            owner = 1 - core if swapped else core
            dy = jnp.where(owner == 0, first, second)
            dz = jnp.where(owner == 0, second, first)
            block = ((y - dy + SIDE) % SIDE * SIDE + (z - dz + SIDE) % SIDE) * CORES + owner
            n = len(loads)
            slot = held.at[pl.ds(n * rows, rows)]
            target = out.at[pl.ds(pl.multiple_of(block * rows, rows), rows)]
            loads.append(pltpu.make_async_copy(source.at[pl.ds(at, rows)], slot, in_sems.at[n]))
            stores.append(pltpu.make_async_copy(slot, target, out_sems.at[n]))
    for load in loads:
        load.start()
    for load, store in zip(loads, stores):
        load.wait()
        store.start()
    for store in stores:
        store.wait()


def place(out, rows, sources, moves):
    count = sum(len(m) for m in moves)
    held = count * rows
    args = list(sources) + ([] if out is None else [out])
    return pl.pallas_call(
        functools.partial(place_kernel, moves, rows),
        in_specs=[ANY] * len(args),
        out_specs=ANY,
        out_shape=jax.ShapeDtypeStruct((COUNT * rows, LANES), sources[0].dtype),
        scratch_shapes=[
            pltpu.VMEM((held, LANES), sources[0].dtype),
            pltpu.SemaphoreType.DMA((count,)),
            pltpu.SemaphoreType.DMA((count,)),
        ],
        input_output_aliases={} if out is None else {len(args) - 1: 0},
        compiler_params=pltpu.CompilerParams(vmem_limit_bytes=held * LANES * 2 + 2 * MIB),
        cost_estimate=pl.CostEstimate(flops=0, bytes_accessed=held * LANES * 4, transcendentals=0),
    )(*args)


def gather(own):
    rows = own.shape[0]
    one, three, two = send(own, 1, 0), send(own, 3, 0), send(own, 2, 0)
    upper = jnp.concatenate([own, one])
    lower = jnp.concatenate([three, two])

    def moves(firsts, second, swapped):
        return [(k * rows, first, second, swapped) for k, first in enumerate(firsts)]

    up, low = (0, 1), (3, 2)
    upper_1, upper_3 = send(upper, 0, 1), send(upper, 0, 3)
    lower_1, lower_3 = send(lower, 0, 1), send(lower, 0, 3)
    upper_2, lower_2 = send(upper_1, 0, 1), send(lower_3, 0, 3)
    out = place(
        None,
        rows,
        [upper, lower, swap(upper), swap(lower)],
        [moves(up, 0, False), moves(low, 0, False), moves(up, 0, True), moves(low, 0, True)],
    )
    near = [upper_1, upper_3, lower_1, lower_3]
    layout = [(up, 1), (up, 3), (low, 1), (low, 3)]
    out = place(out, rows, near, [moves(f, s, False) for f, s in layout])
    out = place(out, rows, [swap(a) for a in near], [moves(f, s, True) for f, s in layout])
    far = [upper_2, lower_2]
    layout = [(up, 2), (low, 2)]
    return place(
        out,
        rows,
        far + [swap(a) for a in far],
        [moves(f, s, False) for f, s in layout] + [moves(f, s, True) for f, s in layout],
    )


def body(grads):
    count = lax.axis_size("rep")
    total = grads.shape[1] * lax.axis_size("shard")
    slab = compact(grads, 8).reshape(count, -1, LANES)
    blocks = lax.all_to_all(slab, "rep", split_axis=0, concat_axis=0, tiled=True)
    gram = partial_gram(blocks, 4)
    everyone = count * lax.axis_size("shard")
    grams = lax.all_to_all(
        jnp.broadcast_to(gram[None], (everyone, 8, LANES)), ("rep", "shard"), 0, 0, tiled=True
    )
    local, weights = aggregate_blocks(grams, blocks, total, 4)
    return (gather(local).reshape(-1), weights[0, :count])


def solution(mesh):
    placed = (P("rep", "shard"),)
    return jax.shard_map(
        body, mesh=mesh, in_specs=placed, out_specs=(P("shard"), P()), check_vma=False
    )
```

```python
import functools

import jax
import jax.numpy as jnp
from jax import lax
from jax.experimental import pallas as pl
from jax.experimental.pallas import tpu as pltpu
from jax.sharding import PartitionSpec as P

ITERS = 4
LANES = 128
PACK = 16
SIDE = 4
CORES = 2
COUNT = SIDE * SIDE * CORES
SHORT = 4
MIB = 1024 * 1024
ANY = pl.BlockSpec(memory_space=pl.ANY)
WHOLE = pl.BlockSpec(memory_space=pltpu.VMEM)


def compact_kernel(parts, piece, x_ref, o_ref, wide, sems):
    size = x_ref.shape[1] // parts
    rows = size // LANES
    loads = [
        pltpu.make_async_copy(x_ref.at[:, pl.ds(i * size, size)], wide.at[:, pl.ds(i * size, size)], sems.at[i])
        for i in range(parts)
    ]
    for load in loads:
        load.start()
    for i in range(parts):
        loads[i].wait()

        @pl.loop(0, rows // piece)
        def _(j):
            at = pl.multiple_of(i * rows + j * piece, piece)
            values = wide[:, pl.ds(pl.multiple_of(at * LANES, piece * LANES), piece * LANES)]
            o_ref[pl.ds(at, piece), :] = values.reshape(piece, LANES)


def compact(grads, parts):
    size = grads.shape[1]
    rows = size // LANES
    return pl.pallas_call(
        functools.partial(compact_kernel, parts, 512),
        in_specs=[ANY],
        out_specs=WHOLE,
        out_shape=jax.ShapeDtypeStruct((rows, LANES), grads.dtype),
        scratch_shapes=[pltpu.VMEM((1, size), grads.dtype), pltpu.SemaphoreType.DMA((parts,))],
        compiler_params=pltpu.CompilerParams(vmem_limit_bytes=40 * MIB),
        cost_estimate=pl.CostEstimate(flops=0, bytes_accessed=6 * size, transcendentals=0),
    )(grads)


def fold(total):
    wide = total.shape[0]
    i = lax.broadcasted_iota(jnp.int32, (wide, wide), 0)
    j = lax.broadcasted_iota(jnp.int32, (wide, wide), 1)
    kept = jnp.where(i % PACK == j % PACK, total, 0.0)
    k = lax.broadcasted_iota(jnp.int32, (wide, LANES), 0)
    s = lax.broadcasted_iota(jnp.int32, (wide, LANES), 1)
    pick = jnp.where(k // PACK == s, 1.0, 0.0)
    columns = jnp.dot(kept, pick, precision=lax.Precision.HIGHEST, preferred_element_type=jnp.float32)
    return columns.reshape(wide // PACK, PACK, LANES).sum(axis=1)


def grid_of(rows):
    row = lax.broadcasted_iota(jnp.int32, (rows, LANES), 0)
    return row, lax.broadcasted_iota(jnp.int32, (rows, LANES), 1)


def distance_kernel(parts, x_ref, o_ref):
    count, rows, _ = x_ref.shape
    half = count // 2
    rows = rows // parts
    product = functools.partial(
        lax.dot_general, dimension_numbers=(((1,), (1,)), ((), ())), preferred_element_type=jnp.float32
    )

    def group(first, part):
        return jnp.concatenate(
            [
                x_ref[first : first + half, part * rows + j * PACK : part * rows + (j + 1) * PACK, :].reshape(
                    half * PACK, LANES
                )
                for j in range(rows // PACK)
            ],
            axis=1,
        )

    totals = None
    for part in range(parts):
        low, high = group(0, part), group(half, part)
        found = (product(low, low), product(high, low), product(high, high))
        totals = found if totals is None else tuple(a + b for a, b in zip(totals, found))
    low_low, high_low, high_high = (fold(t) for t in totals)
    i, s = grid_of(half)

    def squares(gram):
        own = jnp.where(i == s, gram, 0.0)
        return jnp.sum(own, axis=1, keepdims=True), jnp.sum(own, axis=0, keepdims=True)

    low_down, low_across = squares(low_low)
    high_down, high_across = squares(high_high)
    cross = high_down + low_across - 2.0 * high_low
    within_low = low_down + low_across - 2.0 * low_low
    within_high = high_down + high_across - 2.0 * high_high
    cross = jnp.where(s < half, cross, 0.0)
    within = jnp.where(s < i, within_low, jnp.where((s > i) & (s < half), within_high, 0.0))
    both = cross + pltpu.roll(within, half, 1)
    packed = both[:SHORT]
    for q in range(1, half // SHORT):
        packed = packed + pltpu.roll(both[SHORT * q : SHORT * (q + 1)], count * q, 1)
    o_ref[...] = packed


def partial_distances(blocks, parts):
    return pl.pallas_call(
        functools.partial(distance_kernel, parts),
        in_specs=[WHOLE],
        out_specs=WHOLE,
        out_shape=jax.ShapeDtypeStruct((SHORT, LANES), jnp.float32),
        compiler_params=pltpu.CompilerParams(vmem_limit_bytes=32 * MIB),
    )(blocks)


def all_distances(packed, count):
    half = count // 2
    i, s = grid_of(half)
    both = jnp.concatenate([packed] * (half // SHORT), axis=0)
    both = jnp.where(s // count == i // SHORT, both, 0.0)
    both = sum(pltpu.roll(both, count * q, 1) for q in range(1, half // SHORT)) + both
    turned = jnp.concatenate([both, jnp.zeros((LANES - half, LANES), jnp.float32)], axis=0).T
    cross, cross_turned = jnp.where(s < half, both, 0.0), turned[:half]
    within = jnp.where(s < half, pltpu.roll(both, LANES - half, 1), 0.0)
    within_turned = turned[half:count]
    low = jnp.where(s < i, within, jnp.where(s > i, within_turned, 0.0))
    high = jnp.where(s > i, within, jnp.where(s < i, within_turned, 0.0))
    return jnp.concatenate(
        [low + pltpu.roll(cross_turned, half, 1), cross + pltpu.roll(high, half, 1)], axis=0
    )


def weiszfeld(distances, total):
    count = distances.shape[0]
    r, t = grid_of(count)
    same = (t == r).astype(jnp.float32)
    weights = jnp.full((count, 1), 1.0 / count, jnp.float32)
    for _ in range(ITERS):
        across = jnp.sum(same * weights, axis=0, keepdims=True)
        query = jnp.sum(distances * across, axis=1, keepdims=True)
        spread = jnp.sum(weights * query, axis=0, keepdims=True)
        square = jnp.maximum((query - 0.5 * spread) / total, 0.0)
        inverse = 1.0 / jnp.sqrt(square + 1e-06)
        weights = inverse / jnp.sum(inverse, axis=0, keepdims=True)
    return weights, jnp.sum(same * weights, axis=0, keepdims=True)


def aggregate_kernel(total, d_ref, x_ref, o_ref, w_ref, coeffs):
    count, rows, _ = x_ref.shape
    weights, across = weiszfeld(all_distances(d_ref[...].sum(axis=0), count), total)
    w_ref[...] = across
    coeffs[...] = jnp.broadcast_to(weights.astype(jnp.bfloat16).astype(jnp.float32), (count, LANES))
    piece = 32

    @pl.loop(0, rows // piece)
    def _(k):
        at = pl.ds(pl.multiple_of(k * piece, piece), piece)
        sums = [None] * 4
        for r in range(count):
            term = x_ref[r, at, :].astype(jnp.float32) * coeffs[r : r + 1, :]
            sums[r % 4] = term if sums[r % 4] is None else sums[r % 4] + term
        o_ref[at, :] = ((sums[0] + sums[1]) + (sums[2] + sums[3])).astype(o_ref.dtype)


def aggregate_blocks(distances, blocks, total):
    count, rows, _ = blocks.shape
    return pl.pallas_call(
        functools.partial(aggregate_kernel, float(total)),
        in_specs=[WHOLE, WHOLE],
        out_specs=[WHOLE, WHOLE],
        out_shape=[
            jax.ShapeDtypeStruct((rows, LANES), blocks.dtype),
            jax.ShapeDtypeStruct((1, LANES), jnp.float32),
        ],
        scratch_shapes=[pltpu.VMEM((count, LANES), jnp.float32)],
        compiler_params=pltpu.CompilerParams(vmem_limit_bytes=32 * MIB),
    )(distances, blocks)


def send(array, first, second):
    pairs = []
    for y in range(SIDE):
        for z in range(SIDE):
            for core in range(CORES):
                dy, dz = (first, second) if core == 0 else (second, first)
                there = (y + dy) % SIDE * SIDE + (z + dz) % SIDE
                pairs.append(((y * SIDE + z) * CORES + core, there * CORES + core))
    return lax.ppermute(array, "rep", pairs)


def swap(array):
    return lax.ppermute(array, "rep", [(i, i ^ 1) for i in range(COUNT)])


def place_kernel(moves, rows, *refs):
    sources, (out, sems) = refs[: len(moves)], refs[-2:]
    me = lax.axis_index("rep")
    y, z, core = me // (SIDE * CORES), me // CORES % SIDE, me % CORES
    stores = []
    for source, pieces in zip(sources, moves):
        for at, first, second, swapped in pieces:
            owner = 1 - core if swapped else core
            dy = jnp.where(owner == 0, first, second)
            dz = jnp.where(owner == 0, second, first)
            block = ((y - dy + SIDE) % SIDE * SIDE + (z - dz + SIDE) % SIDE) * CORES + owner
            target = out.at[pl.ds(pl.multiple_of(block * rows, rows), rows)]
            stores.append(pltpu.make_async_copy(source.at[pl.ds(at, rows)], target, sems.at[len(stores)]))
    for store in stores:
        store.start()
    for store in stores:
        store.wait()


def place(out, rows, sources, moves):
    count = sum(len(m) for m in moves)
    args = list(sources) + ([] if out is None else [out])
    return pl.pallas_call(
        functools.partial(place_kernel, moves, rows),
        in_specs=[WHOLE] * len(sources) + ([] if out is None else [ANY]),
        out_specs=ANY,
        out_shape=jax.ShapeDtypeStruct((COUNT * rows, LANES), sources[0].dtype),
        scratch_shapes=[pltpu.SemaphoreType.DMA((count,))],
        input_output_aliases={} if out is None else {len(args) - 1: 0},
        compiler_params=pltpu.CompilerParams(vmem_limit_bytes=16 * MIB),
        cost_estimate=pl.CostEstimate(flops=0, bytes_accessed=count * rows * LANES * 2, transcendentals=0),
    )(*args)


def after(array, *others):
    return lax.optimization_barrier((array, *others))[0]


def gather(own):
    rows = own.shape[0]

    def moves(firsts, second, swapped):
        return [(k * rows, first, second, swapped) for k, first in enumerate(firsts)]

    up, low = (0, 1), (3, 2)
    one, three, two = send(own, 1, 0), send(own, 3, 0), send(own, 2, 0)
    upper = jnp.concatenate([own, one])
    lower = jnp.concatenate([three, two])
    upper_1, upper_3 = send(upper, 0, 1), send(upper, 0, 3)
    lower_1, lower_3 = send(lower, 0, 1), send(lower, 0, 3)
    upper_2, lower_2 = send(upper_1, 0, 1), send(lower_3, 0, 3)
    out = place(
        None,
        rows,
        [upper, lower, swap(upper), swap(lower)],
        [moves(up, 0, False), moves(low, 0, False), moves(up, 0, True), moves(low, 0, True)],
    )
    swapped = [swap(a) for a in (upper_1, upper_3, after(lower_1, out), after(lower_3, out))]
    layout = [(up, 1), (up, 3), (low, 1), (low, 3)]
    out = place(out, rows, [upper_1, upper_3, lower_1, lower_3], [moves(f, s, False) for f, s in layout])
    far = [swap(after(upper_2, out)), swap(after(lower_2, out))]
    out = place(
        out,
        rows,
        swapped + [upper_2, lower_2],
        [moves(f, s, True) for f, s in layout] + [moves(up, 2, False), moves(low, 2, False)],
    )
    return place(out, rows, far, [moves(up, 2, True), moves(low, 2, True)])


def body(grads):
    count = lax.axis_size("rep")
    total = grads.shape[1] * lax.axis_size("shard")
    slab = compact(grads, 8).reshape(count, -1, LANES)
    blocks = lax.all_to_all(slab, "rep", split_axis=0, concat_axis=0, tiled=True)
    part = partial_distances(blocks, 4)
    everyone = count * lax.axis_size("shard")
    distances = lax.all_to_all(
        jnp.broadcast_to(part[None], (everyone, SHORT, LANES)), ("rep", "shard"), 0, 0, tiled=True
    )
    local, weights = aggregate_blocks(distances, blocks, total)
    return (gather(local).reshape(-1), weights[0, :count])


def solution(mesh):
    placed = (P("rep", "shard"),)
    return jax.shard_map(
        body, mesh=mesh, in_specs=placed, out_specs=(P("shard"), P()), check_vma=False
    )
```

```python
import functools

import jax
import jax.numpy as jnp
from jax import lax
from jax.experimental import pallas as pl
from jax.experimental.pallas import tpu as pltpu
from jax.sharding import PartitionSpec as P

ITERS = 4
LANES = 128
PACK = 16
SIDE = 4
CORES = 2
COUNT = SIDE * SIDE * CORES
SHORT = 4
MIB = 1024 * 1024
ANY = pl.BlockSpec(memory_space=pl.ANY)
WHOLE = pl.BlockSpec(memory_space=pltpu.VMEM)


def compact_kernel(parts, piece, x_ref, o_ref, wide, sems):
    size = x_ref.shape[1] // parts
    rows = size // LANES
    loads = [
        pltpu.make_async_copy(x_ref.at[:, pl.ds(i * size, size)], wide.at[:, pl.ds(i * size, size)], sems.at[i])
        for i in range(parts)
    ]
    for load in loads:
        load.start()
    for i in range(parts):
        loads[i].wait()

        @pl.loop(0, rows // piece)
        def _(j):
            at = pl.multiple_of(i * rows + j * piece, piece)
            values = wide[:, pl.ds(pl.multiple_of(at * LANES, piece * LANES), piece * LANES)]
            o_ref[pl.ds(at, piece), :] = values.reshape(piece, LANES)


def compact(grads, parts):
    size = grads.shape[1]
    rows = size // LANES
    return pl.pallas_call(
        functools.partial(compact_kernel, parts, 512),
        in_specs=[ANY],
        out_specs=WHOLE,
        out_shape=jax.ShapeDtypeStruct((rows, LANES), grads.dtype),
        scratch_shapes=[pltpu.VMEM((1, size), grads.dtype), pltpu.SemaphoreType.DMA((parts,))],
        compiler_params=pltpu.CompilerParams(vmem_limit_bytes=40 * MIB),
        cost_estimate=pl.CostEstimate(flops=0, bytes_accessed=6 * size, transcendentals=0),
    )(grads)


def fold(total):
    wide = total.shape[0]
    i = lax.broadcasted_iota(jnp.int32, (wide, wide), 0)
    j = lax.broadcasted_iota(jnp.int32, (wide, wide), 1)
    kept = jnp.where(i % PACK == j % PACK, total, 0.0)
    k = lax.broadcasted_iota(jnp.int32, (wide, LANES), 0)
    s = lax.broadcasted_iota(jnp.int32, (wide, LANES), 1)
    pick = jnp.where(k // PACK == s, 1.0, 0.0)
    columns = jnp.dot(kept, pick, precision=lax.Precision.HIGHEST, preferred_element_type=jnp.float32)
    return columns.reshape(wide // PACK, PACK, LANES).sum(axis=1)


def grid_of(rows):
    row = lax.broadcasted_iota(jnp.int32, (rows, LANES), 0)
    return row, lax.broadcasted_iota(jnp.int32, (rows, LANES), 1)


def distance_kernel(parts, x_ref, o_ref):
    count, rows, _ = x_ref.shape
    half = count // 2
    rows = rows // parts
    product = functools.partial(
        lax.dot_general, dimension_numbers=(((1,), (1,)), ((), ())), preferred_element_type=jnp.float32
    )

    def group(first, part):
        return jnp.concatenate(
            [
                x_ref[first : first + half, part * rows + j * PACK : part * rows + (j + 1) * PACK, :].reshape(
                    half * PACK, LANES
                )
                for j in range(rows // PACK)
            ],
            axis=1,
        )

    totals = None
    for part in range(parts):
        low, high = group(0, part), group(half, part)
        found = (product(low, low), product(high, low), product(high, high))
        totals = found if totals is None else tuple(a + b for a, b in zip(totals, found))
    low_low, high_low, high_high = (fold(t) for t in totals)
    i, s = grid_of(half)

    def squares(gram):
        own = jnp.where(i == s, gram, 0.0)
        return jnp.sum(own, axis=1, keepdims=True), jnp.sum(own, axis=0, keepdims=True)

    low_down, low_across = squares(low_low)
    high_down, high_across = squares(high_high)
    cross = high_down + low_across - 2.0 * high_low
    within_low = low_down + low_across - 2.0 * low_low
    within_high = high_down + high_across - 2.0 * high_high
    cross = jnp.where(s < half, cross, 0.0)
    within = jnp.where(s < i, within_low, jnp.where((s > i) & (s < half), within_high, 0.0))
    both = cross + pltpu.roll(within, half, 1)
    packed = both[:SHORT]
    for q in range(1, half // SHORT):
        packed = packed + pltpu.roll(both[SHORT * q : SHORT * (q + 1)], count * q, 1)
    o_ref[...] = packed


def partial_distances(blocks, parts):
    return pl.pallas_call(
        functools.partial(distance_kernel, parts),
        in_specs=[WHOLE],
        out_specs=WHOLE,
        out_shape=jax.ShapeDtypeStruct((SHORT, LANES), jnp.float32),
        compiler_params=pltpu.CompilerParams(vmem_limit_bytes=32 * MIB),
    )(blocks)


def all_distances(packed, count):
    half = count // 2
    i, s = grid_of(half)
    both = jnp.concatenate([packed] * (half // SHORT), axis=0)
    both = jnp.where(s // count == i // SHORT, both, 0.0)
    both = sum(pltpu.roll(both, count * q, 1) for q in range(1, half // SHORT)) + both
    turned = jnp.concatenate([both, jnp.zeros((LANES - half, LANES), jnp.float32)], axis=0).T
    cross, cross_turned = jnp.where(s < half, both, 0.0), turned[:half]
    within = jnp.where(s < half, pltpu.roll(both, LANES - half, 1), 0.0)
    within_turned = turned[half:count]
    low = jnp.where(s < i, within, jnp.where(s > i, within_turned, 0.0))
    high = jnp.where(s > i, within, jnp.where(s < i, within_turned, 0.0))
    return jnp.concatenate(
        [low + pltpu.roll(cross_turned, half, 1), cross + pltpu.roll(high, half, 1)], axis=0
    )


def weiszfeld(distances, total):
    count = distances.shape[0]
    r, t = grid_of(count)
    same = (t == r).astype(jnp.float32)
    weights = jnp.full((count, 1), 1.0 / count, jnp.float32)
    for _ in range(ITERS):
        across = jnp.sum(same * weights, axis=0, keepdims=True)
        query = jnp.sum(distances * across, axis=1, keepdims=True)
        spread = jnp.sum(weights * query, axis=0, keepdims=True)
        square = jnp.maximum((query - 0.5 * spread) / total, 0.0)
        inverse = 1.0 / jnp.sqrt(square + 1e-06)
        weights = inverse / jnp.sum(inverse, axis=0, keepdims=True)
    return weights, jnp.sum(same * weights, axis=0, keepdims=True)


def aggregate_kernel(total, d_ref, x_ref, o_ref, w_ref, coeffs):
    count, rows, _ = x_ref.shape
    weights, across = weiszfeld(all_distances(d_ref[...].sum(axis=0), count), total)
    w_ref[...] = across
    coeffs[...] = jnp.broadcast_to(weights.astype(jnp.bfloat16).astype(jnp.float32), (count, LANES))
    piece = 32

    @pl.loop(0, rows // piece)
    def _(k):
        at = pl.ds(pl.multiple_of(k * piece, piece), piece)
        sums = [None] * 4
        for r in range(count):
            term = x_ref[r, at, :].astype(jnp.float32) * coeffs[r : r + 1, :]
            sums[r % 4] = term if sums[r % 4] is None else sums[r % 4] + term
        o_ref[at, :] = ((sums[0] + sums[1]) + (sums[2] + sums[3])).astype(o_ref.dtype)


def aggregate_blocks(distances, blocks, total):
    count, rows, _ = blocks.shape
    return pl.pallas_call(
        functools.partial(aggregate_kernel, float(total)),
        in_specs=[WHOLE, WHOLE],
        out_specs=[WHOLE, WHOLE],
        out_shape=[
            jax.ShapeDtypeStruct((rows, LANES), blocks.dtype),
            jax.ShapeDtypeStruct((1, LANES), jnp.float32),
        ],
        scratch_shapes=[pltpu.VMEM((count, LANES), jnp.float32)],
        compiler_params=pltpu.CompilerParams(vmem_limit_bytes=32 * MIB),
    )(distances, blocks)


def send(array, first, second):
    pairs = []
    for y in range(SIDE):
        for z in range(SIDE):
            for core in range(CORES):
                dy, dz = (first, second) if core == 0 else (second, first)
                there = (y + dy) % SIDE * SIDE + (z + dz) % SIDE
                pairs.append(((y * SIDE + z) * CORES + core, there * CORES + core))
    return lax.ppermute(array, "rep", pairs)


def swap(array):
    return lax.ppermute(array, "rep", [(i, i ^ 1) for i in range(COUNT)])


def place_kernel(moves, rows, *refs):
    sources, (out, sems) = refs[: len(moves)], refs[-2:]
    me = lax.axis_index("rep")
    y, z, core = me // (SIDE * CORES), me // CORES % SIDE, me % CORES
    stores = []
    for source, pieces in zip(sources, moves):
        for at, first, second, swapped in pieces:
            owner = 1 - core if swapped else core
            dy = jnp.where(owner == 0, first, second)
            dz = jnp.where(owner == 0, second, first)
            block = ((y - dy + SIDE) % SIDE * SIDE + (z - dz + SIDE) % SIDE) * CORES + owner
            target = out.at[pl.ds(pl.multiple_of(block * rows, rows), rows)]
            stores.append(pltpu.make_async_copy(source.at[pl.ds(at, rows)], target, sems.at[len(stores)]))
    for store in stores:
        store.start()
    for store in stores:
        store.wait()


def place(out, rows, sources, moves):
    count = sum(len(m) for m in moves)
    args = list(sources) + ([] if out is None else [out])
    return pl.pallas_call(
        functools.partial(place_kernel, moves, rows),
        in_specs=[WHOLE] * len(sources) + ([] if out is None else [ANY]),
        out_specs=ANY,
        out_shape=jax.ShapeDtypeStruct((COUNT * rows, LANES), sources[0].dtype),
        scratch_shapes=[pltpu.SemaphoreType.DMA((count,))],
        input_output_aliases={} if out is None else {len(args) - 1: 0},
        compiler_params=pltpu.CompilerParams(vmem_limit_bytes=16 * MIB),
        cost_estimate=pl.CostEstimate(flops=0, bytes_accessed=count * rows * LANES * 2, transcendentals=0),
    )(*args)


def after(array, *others):
    return lax.optimization_barrier((array, *others))[0]


def gather(own, *early):
    rows = own.shape[0]

    def moves(firsts, second, swapped):
        return [(k * rows, first, second, swapped) for k, first in enumerate(firsts)]

    up, low = (0, 1), (3, 2)
    one, three, two = send(own, 1, 0), send(own, 3, 0), send(own, 2, 0)
    upper = jnp.concatenate([own, one])
    lower = jnp.concatenate([three, two])
    upper_1, upper_3 = send(upper, 0, 1), send(upper, 0, 3)
    lower_1, lower_3 = send(lower, 0, 1), send(lower, 0, 3)
    upper_2, lower_2 = send(upper_3, 0, 3), send(lower_1, 0, 1)
    out = place(
        None,
        rows,
        [upper, lower, swap(upper), swap(lower)],
        [moves(up, 0, False), moves(low, 0, False), moves(up, 0, True), moves(low, 0, True)],
    )
    swapped = [swap(a) for a in (upper_1, upper_3, after(lower_1, out, *early), after(lower_3, out))]
    layout = [(up, 1), (up, 3), (low, 1), (low, 3)]
    out = place(out, rows, [upper_1, upper_3, lower_1, lower_3], [moves(f, s, False) for f, s in layout])
    far = [swap(after(upper_2, out)), swap(after(lower_2, out))]
    out = place(
        out,
        rows,
        swapped + [upper_2, lower_2],
        [moves(f, s, True) for f, s in layout] + [moves(up, 2, False), moves(low, 2, False)],
    )
    return place(out, rows, far, [moves(up, 2, True), moves(low, 2, True)])


def body(grads):
    count = lax.axis_size("rep")
    total = grads.shape[1] * lax.axis_size("shard")
    slab = compact(grads, 8).reshape(count, -1, LANES)
    blocks = lax.all_to_all(slab, "rep", split_axis=0, concat_axis=0, tiled=True)
    part = partial_distances(blocks, 1)
    everyone = count * lax.axis_size("shard")
    distances = lax.all_to_all(
        jnp.broadcast_to(part[None], (everyone, SHORT, LANES)), ("rep", "shard"), 0, 0, tiled=True
    )
    local, weights = aggregate_blocks(distances, blocks, total)
    weights = weights[0, :count]
    return (gather(local, weights).reshape(-1), weights)


def solution(mesh):
    placed = (P("rep", "shard"),)
    return jax.shard_map(
        body, mesh=mesh, in_specs=placed, out_specs=(P("shard"), P()), check_vma=False
    )
```

```python
import functools

import jax
import jax.numpy as jnp
from jax import lax
from jax.experimental import pallas as pl
from jax.experimental.pallas import tpu as pltpu
from jax.sharding import PartitionSpec as P

ITERS = 4
LANES = 128
PACK = 16
SIDE = 4
CORES = 2
COUNT = SIDE * SIDE * CORES
SHORT = 4
MIB = 1024 * 1024
ANY = pl.BlockSpec(memory_space=pl.ANY)
WHOLE = pl.BlockSpec(memory_space=pltpu.VMEM)


def compact_kernel(parts, piece, x_ref, o_ref, wide, sems):
    size = x_ref.shape[1] // parts
    rows = size // LANES
    loads = [
        pltpu.make_async_copy(x_ref.at[:, pl.ds(i * size, size)], wide.at[:, pl.ds(i * size, size)], sems.at[i])
        for i in range(parts)
    ]
    for load in loads:
        load.start()
    for i in range(parts):
        loads[i].wait()

        @pl.loop(0, rows // piece)
        def _(j):
            at = pl.multiple_of(i * rows + j * piece, piece)
            values = wide[:, pl.ds(pl.multiple_of(at * LANES, piece * LANES), piece * LANES)]
            o_ref[pl.ds(at, piece), :] = values.reshape(piece, LANES)


def compact(grads, parts):
    size = grads.shape[1]
    rows = size // LANES
    return pl.pallas_call(
        functools.partial(compact_kernel, parts, 512),
        in_specs=[ANY],
        out_specs=WHOLE,
        out_shape=jax.ShapeDtypeStruct((rows, LANES), grads.dtype),
        scratch_shapes=[pltpu.VMEM((1, size), grads.dtype), pltpu.SemaphoreType.DMA((parts,))],
        compiler_params=pltpu.CompilerParams(vmem_limit_bytes=40 * MIB),
        cost_estimate=pl.CostEstimate(flops=0, bytes_accessed=6 * size, transcendentals=0),
    )(grads)


def fold(totals):
    wide = totals[0].shape[0]
    i = lax.broadcasted_iota(jnp.int32, (wide, wide), 0)
    j = lax.broadcasted_iota(jnp.int32, (wide, wide), 1)
    same = i % PACK == j % PACK
    groups = wide // PACK
    rows = [jnp.where(same, total, 0.0).reshape(groups, PACK, wide).sum(axis=1) for total in totals]
    k = lax.broadcasted_iota(jnp.int32, (wide, LANES), 0)
    s = lax.broadcasted_iota(jnp.int32, (wide, LANES), 1)
    pick = jnp.where(k // PACK == s, 1.0, 0.0)
    folded = jnp.dot(
        jnp.concatenate(rows, axis=0), pick, precision=lax.Precision.HIGHEST, preferred_element_type=jnp.float32
    )
    return [folded[n * groups : (n + 1) * groups] for n in range(len(totals))]


def grid_of(rows):
    row = lax.broadcasted_iota(jnp.int32, (rows, LANES), 0)
    return row, lax.broadcasted_iota(jnp.int32, (rows, LANES), 1)


def distance_kernel(parts, x_ref, o_ref):
    count, rows, _ = x_ref.shape
    half = count // 2
    rows = rows // parts
    product = functools.partial(
        lax.dot_general, dimension_numbers=(((1,), (1,)), ((), ())), preferred_element_type=jnp.float32
    )

    def group(first, part):
        return jnp.concatenate(
            [
                x_ref[first : first + half, part * rows + j * PACK : part * rows + (j + 1) * PACK, :].reshape(
                    half * PACK, LANES
                )
                for j in range(rows // PACK)
            ],
            axis=1,
        )

    totals = None
    for part in range(parts):
        low, high = group(0, part), group(half, part)
        found = (product(low, low), product(high, low), product(high, high))
        totals = found if totals is None else tuple(a + b for a, b in zip(totals, found))
    low_low, high_low, high_high = fold(totals)
    i, s = grid_of(half)

    def squares(gram):
        own = jnp.where(i == s, gram, 0.0)
        return jnp.sum(own, axis=1, keepdims=True), jnp.sum(own, axis=0, keepdims=True)

    low_down, low_across = squares(low_low)
    high_down, high_across = squares(high_high)
    cross = high_down + low_across - 2.0 * high_low
    within_low = low_down + low_across - 2.0 * low_low
    within_high = high_down + high_across - 2.0 * high_high
    cross = jnp.where(s < half, cross, 0.0)
    within = jnp.where(s < i, within_low, jnp.where((s > i) & (s < half), within_high, 0.0))
    both = cross + pltpu.roll(within, half, 1)
    packed = both[:SHORT]
    for q in range(1, half // SHORT):
        packed = packed + pltpu.roll(both[SHORT * q : SHORT * (q + 1)], count * q, 1)
    o_ref[...] = packed


def partial_distances(blocks, parts):
    return pl.pallas_call(
        functools.partial(distance_kernel, parts),
        in_specs=[WHOLE],
        out_specs=WHOLE,
        out_shape=jax.ShapeDtypeStruct((SHORT, LANES), jnp.float32),
        compiler_params=pltpu.CompilerParams(vmem_limit_bytes=32 * MIB),
    )(blocks)


def all_distances(packed, count):
    half = count // 2
    i, s = grid_of(half)
    both = jnp.concatenate([packed] * (half // SHORT), axis=0)
    both = jnp.where(s // count == i // SHORT, both, 0.0)
    both = sum(pltpu.roll(both, count * q, 1) for q in range(1, half // SHORT)) + both
    turned = jnp.concatenate([both, jnp.zeros((LANES - half, LANES), jnp.float32)], axis=0).T
    cross, cross_turned = jnp.where(s < half, both, 0.0), turned[:half]
    within = jnp.where(s < half, pltpu.roll(both, LANES - half, 1), 0.0)
    within_turned = turned[half:count]
    low = jnp.where(s < i, within, jnp.where(s > i, within_turned, 0.0))
    high = jnp.where(s > i, within, jnp.where(s < i, within_turned, 0.0))
    return jnp.concatenate(
        [low + pltpu.roll(cross_turned, half, 1), cross + pltpu.roll(high, half, 1)], axis=0
    )


def weiszfeld(distances, total):
    count = distances.shape[0]
    r, t = grid_of(count)
    same = (t == r).astype(jnp.float32)
    weights = jnp.full((count, 1), 1.0 / count, jnp.float32)
    for _ in range(ITERS):
        across = jnp.sum(same * weights, axis=0, keepdims=True)
        query = jnp.sum(distances * across, axis=1, keepdims=True)
        spread = jnp.sum(weights * query, axis=0, keepdims=True)
        square = jnp.maximum((query - 0.5 * spread) / total, 0.0)
        inverse = 1.0 / jnp.sqrt(square + 1e-06)
        weights = inverse / jnp.sum(inverse, axis=0, keepdims=True)
    return weights, jnp.sum(same * weights, axis=0, keepdims=True)


def aggregate_kernel(total, d_ref, x_ref, o_ref, w_ref, coeffs):
    count, rows, _ = x_ref.shape
    weights, across = weiszfeld(all_distances(d_ref[...].sum(axis=0), count), total)
    w_ref[...] = across
    coeffs[...] = jnp.broadcast_to(weights.astype(jnp.bfloat16).astype(jnp.float32), (count, LANES))
    piece = 32

    @pl.loop(0, rows // piece)
    def _(k):
        at = pl.ds(pl.multiple_of(k * piece, piece), piece)
        sums = [None] * 4
        for r in range(count):
            term = x_ref[r, at, :].astype(jnp.float32) * coeffs[r : r + 1, :]
            sums[r % 4] = term if sums[r % 4] is None else sums[r % 4] + term
        o_ref[at, :] = ((sums[0] + sums[1]) + (sums[2] + sums[3])).astype(o_ref.dtype)


def aggregate_blocks(distances, blocks, total):
    count, rows, _ = blocks.shape
    return pl.pallas_call(
        functools.partial(aggregate_kernel, float(total)),
        in_specs=[WHOLE, WHOLE],
        out_specs=[WHOLE, WHOLE],
        out_shape=[
            jax.ShapeDtypeStruct((rows, LANES), blocks.dtype),
            jax.ShapeDtypeStruct((1, LANES), jnp.float32),
        ],
        scratch_shapes=[pltpu.VMEM((count, LANES), jnp.float32)],
        compiler_params=pltpu.CompilerParams(vmem_limit_bytes=32 * MIB),
    )(distances, blocks)


def send(array, first, second):
    pairs = []
    for y in range(SIDE):
        for z in range(SIDE):
            for core in range(CORES):
                dy, dz = (first, second) if core == 0 else (second, first)
                there = (y + dy) % SIDE * SIDE + (z + dz) % SIDE
                pairs.append(((y * SIDE + z) * CORES + core, there * CORES + core))
    return lax.ppermute(array, "rep", pairs)


def swap(array):
    return lax.ppermute(array, "rep", [(i, i ^ 1) for i in range(COUNT)])


def place_kernel(moves, rows, *refs):
    sources, (out, sems) = refs[: len(moves)], refs[-2:]
    me = lax.axis_index("rep")
    y, z, core = me // (SIDE * CORES), me // CORES % SIDE, me % CORES
    stores = []
    for source, pieces in zip(sources, moves):
        for at, first, second, swapped in pieces:
            owner = 1 - core if swapped else core
            dy = jnp.where(owner == 0, first, second)
            dz = jnp.where(owner == 0, second, first)
            block = ((y - dy + SIDE) % SIDE * SIDE + (z - dz + SIDE) % SIDE) * CORES + owner
            target = out.at[pl.ds(pl.multiple_of(block * rows, rows), rows)]
            stores.append(pltpu.make_async_copy(source.at[pl.ds(at, rows)], target, sems.at[len(stores)]))
    for store in stores:
        store.start()
    for store in stores:
        store.wait()


def place(out, rows, sources, moves):
    count = sum(len(m) for m in moves)
    args = list(sources) + ([] if out is None else [out])
    return pl.pallas_call(
        functools.partial(place_kernel, moves, rows),
        in_specs=[WHOLE] * len(sources) + ([] if out is None else [ANY]),
        out_specs=ANY,
        out_shape=jax.ShapeDtypeStruct((COUNT * rows, LANES), sources[0].dtype),
        scratch_shapes=[pltpu.SemaphoreType.DMA((count,))],
        input_output_aliases={} if out is None else {len(args) - 1: 0},
        compiler_params=pltpu.CompilerParams(vmem_limit_bytes=16 * MIB),
        cost_estimate=pl.CostEstimate(flops=0, bytes_accessed=count * rows * LANES * 2, transcendentals=0),
    )(*args)


def after(array, *others):
    return lax.optimization_barrier((array, *others))[0]


def gather(own, *early):
    rows = own.shape[0]

    def moves(firsts, second, swapped):
        return [(k * rows, first, second, swapped) for k, first in enumerate(firsts)]

    up, low = (0, 1), (3, 2)
    one, three, two = send(own, 1, 0), send(own, 3, 0), send(own, 2, 0)
    upper = jnp.concatenate([own, one])
    lower = jnp.concatenate([three, two])
    upper_1, upper_3 = send(upper, 0, 1), send(upper, 0, 3)
    lower_1, lower_3 = send(lower, 0, 1), send(lower, 0, 3)
    upper_2, lower_2 = send(upper_3, 0, 3), send(lower_1, 0, 1)
    out = place(
        None,
        rows,
        [upper, lower, swap(upper), swap(lower)],
        [moves(up, 0, False), moves(low, 0, False), moves(up, 0, True), moves(low, 0, True)],
    )
    swapped = [swap(a) for a in (upper_1, upper_3, after(lower_1, out, *early), after(lower_3, out))]
    layout = [(up, 1), (up, 3), (low, 1), (low, 3)]
    out = place(out, rows, [upper_1, upper_3, lower_1, lower_3], [moves(f, s, False) for f, s in layout])
    far = [swap(after(upper_2, out)), swap(after(lower_2, out))]
    out = place(
        out,
        rows,
        swapped + [upper_2, lower_2],
        [moves(f, s, True) for f, s in layout] + [moves(up, 2, False), moves(low, 2, False)],
    )
    return place(out, rows, far, [moves(up, 2, True), moves(low, 2, True)])


def body(grads):
    count = lax.axis_size("rep")
    total = grads.shape[1] * lax.axis_size("shard")
    slab = compact(grads, 8).reshape(count, -1, LANES)
    blocks = lax.all_to_all(slab, "rep", split_axis=0, concat_axis=0, tiled=True)
    part = partial_distances(blocks, 1)
    everyone = count * lax.axis_size("shard")
    distances = lax.all_to_all(
        jnp.broadcast_to(part[None], (everyone, SHORT, LANES)), ("rep", "shard"), 0, 0, tiled=True
    )
    local, weights = aggregate_blocks(distances, blocks, total)
    weights = weights[0, :count]
    return (gather(local, weights).reshape(-1), weights)


def solution(mesh):
    placed = (P("rep", "shard"),)
    return jax.shard_map(
        body, mesh=mesh, in_specs=placed, out_specs=(P("shard"), P()), check_vma=False
    )
```

```python
import functools

import jax
import jax.numpy as jnp
from jax import lax
from jax.experimental import pallas as pl
from jax.experimental.pallas import tpu as pltpu
from jax.sharding import PartitionSpec as P

ITERS = 4
LANES = 128
PACK = 16
SIDE = 4
CORES = 2
COUNT = SIDE * SIDE * CORES
SHORT = 4
MIB = 1024 * 1024
ANY = pl.BlockSpec(memory_space=pl.ANY)
WHOLE = pl.BlockSpec(memory_space=pltpu.VMEM)


def compact_kernel(parts, piece, x_ref, o_ref, wide, sems):
    size = x_ref.shape[1] // parts
    rows = size // LANES
    loads = [
        pltpu.make_async_copy(x_ref.at[:, pl.ds(i * size, size)], wide.at[:, pl.ds(i * size, size)], sems.at[i])
        for i in range(parts)
    ]
    for load in loads:
        load.start()
    for i in range(parts):
        loads[i].wait()

        @pl.loop(0, rows // piece)
        def _(j):
            at = pl.multiple_of(i * rows + j * piece, piece)
            values = wide[:, pl.ds(pl.multiple_of(at * LANES, piece * LANES), piece * LANES)]
            o_ref[pl.ds(at, piece), :] = values.reshape(piece, LANES)


def compact(grads, parts):
    size = grads.shape[1]
    rows = size // LANES
    return pl.pallas_call(
        functools.partial(compact_kernel, parts, 512),
        in_specs=[ANY],
        out_specs=WHOLE,
        out_shape=jax.ShapeDtypeStruct((rows, LANES), grads.dtype),
        scratch_shapes=[pltpu.VMEM((1, size), grads.dtype), pltpu.SemaphoreType.DMA((parts,))],
        compiler_params=pltpu.CompilerParams(vmem_limit_bytes=40 * MIB),
        cost_estimate=pl.CostEstimate(flops=0, bytes_accessed=6 * size, transcendentals=0),
    )(grads)


def fold(totals):
    wide = totals[0].shape[0]
    i = lax.broadcasted_iota(jnp.int32, (wide, wide), 0)
    j = lax.broadcasted_iota(jnp.int32, (wide, wide), 1)
    same = i % PACK == j % PACK
    groups = wide // PACK
    rows = [jnp.where(same, total, 0.0).reshape(groups, PACK, wide).sum(axis=1) for total in totals]
    k = lax.broadcasted_iota(jnp.int32, (wide, LANES), 0)
    s = lax.broadcasted_iota(jnp.int32, (wide, LANES), 1)
    pick = jnp.where(k // PACK == s, 1.0, 0.0)
    folded = jnp.dot(
        jnp.concatenate(rows, axis=0), pick, precision=lax.Precision.HIGHEST, preferred_element_type=jnp.float32
    )
    return [folded[n * groups : (n + 1) * groups] for n in range(len(totals))]


def grid_of(rows):
    row = lax.broadcasted_iota(jnp.int32, (rows, LANES), 0)
    return row, lax.broadcasted_iota(jnp.int32, (rows, LANES), 1)


def distance_kernel(parts, x_ref, o_ref):
    count, rows, _ = x_ref.shape
    half = count // 2
    rows = rows // parts
    product = functools.partial(
        lax.dot_general, dimension_numbers=(((1,), (1,)), ((), ())), preferred_element_type=jnp.float32
    )

    def group(first, part):
        return jnp.concatenate(
            [
                x_ref[first : first + half, part * rows + j * PACK : part * rows + (j + 1) * PACK, :].reshape(
                    half * PACK, LANES
                )
                for j in range(rows // PACK)
            ],
            axis=1,
        )

    totals = None
    for part in range(parts):
        low, high = group(0, part), group(half, part)
        found = (product(low, low), product(high, low), product(high, high))
        totals = found if totals is None else tuple(a + b for a, b in zip(totals, found))
    low_low, high_low, high_high = fold(totals)
    i, s = grid_of(half)

    def squares(gram):
        own = jnp.where(i == s, gram, 0.0)
        return jnp.sum(own, axis=1, keepdims=True), jnp.sum(own, axis=0, keepdims=True)

    low_down, low_across = squares(low_low)
    high_down, high_across = squares(high_high)
    cross = high_down + low_across - 2.0 * high_low
    within_low = low_down + low_across - 2.0 * low_low
    within_high = high_down + high_across - 2.0 * high_high
    cross = jnp.where(s < half, cross, 0.0)
    within = jnp.where(s < i, within_low, jnp.where((s > i) & (s < half), within_high, 0.0))
    both = cross + pltpu.roll(within, half, 1)
    packed = both[:SHORT]
    for q in range(1, half // SHORT):
        packed = packed + pltpu.roll(both[SHORT * q : SHORT * (q + 1)], count * q, 1)
    o_ref[...] = packed


def partial_distances(blocks, parts):
    return pl.pallas_call(
        functools.partial(distance_kernel, parts),
        in_specs=[WHOLE],
        out_specs=WHOLE,
        out_shape=jax.ShapeDtypeStruct((SHORT, LANES), jnp.float32),
        compiler_params=pltpu.CompilerParams(vmem_limit_bytes=32 * MIB),
    )(blocks)


def all_distances(packed, count):
    half = count // 2
    i, s = grid_of(half)
    both = jnp.concatenate([packed] * (half // SHORT), axis=0)
    both = jnp.where(s // count == i // SHORT, both, 0.0)
    both = sum(pltpu.roll(both, count * q, 1) for q in range(1, half // SHORT)) + both
    turned = jnp.concatenate([both, jnp.zeros((LANES - half, LANES), jnp.float32)], axis=0).T
    cross, cross_turned = jnp.where(s < half, both, 0.0), turned[:half]
    within = jnp.where(s < half, pltpu.roll(both, LANES - half, 1), 0.0)
    within_turned = turned[half:count]
    low = jnp.where(s < i, within, jnp.where(s > i, within_turned, 0.0))
    high = jnp.where(s > i, within, jnp.where(s < i, within_turned, 0.0))
    return jnp.concatenate(
        [low + pltpu.roll(cross_turned, half, 1), cross + pltpu.roll(high, half, 1)], axis=0
    )


def weiszfeld(distances, total):
    count = distances.shape[0]
    r, t = grid_of(count)
    same = (t == r).astype(jnp.float32)
    weights = jnp.full((count, 1), 1.0 / count, jnp.float32)
    for _ in range(ITERS):
        across = jnp.sum(same * weights, axis=0, keepdims=True)
        query = jnp.sum(distances * across, axis=1, keepdims=True)
        spread = jnp.sum(weights * query, axis=0, keepdims=True)
        square = jnp.maximum((query - 0.5 * spread) / total, 0.0)
        inverse = 1.0 / jnp.sqrt(square + 1e-06)
        weights = inverse / jnp.sum(inverse, axis=0, keepdims=True)
    return weights, jnp.sum(same * weights, axis=0, keepdims=True)


def add_up(ref, ways=8):
    each = ref.shape[0] // ways
    sums = [ref[n * each] for n in range(ways)]
    for k in range(1, each):
        sums = [total + ref[n * each + k] for n, total in enumerate(sums)]
    while len(sums) > 1:
        sums = [a + b for a, b in zip(sums[::2], sums[1::2])]
    return sums[0]


def aggregate_kernel(total, d_ref, x_ref, o_ref, w_ref, coeffs):
    count, rows, _ = x_ref.shape
    weights, across = weiszfeld(all_distances(add_up(d_ref), count), total)
    w_ref[...] = across
    coeffs[...] = jnp.broadcast_to(weights.astype(jnp.bfloat16).astype(jnp.float32), (count, LANES))
    piece = 64

    @pl.loop(0, rows // piece)
    def _(k):
        at = pl.ds(pl.multiple_of(k * piece, piece), piece)
        sums = [None] * 4
        for r in range(count):
            term = x_ref[r, at, :].astype(jnp.float32) * coeffs[r : r + 1, :]
            sums[r % 4] = term if sums[r % 4] is None else sums[r % 4] + term
        o_ref[at, :] = ((sums[0] + sums[1]) + (sums[2] + sums[3])).astype(o_ref.dtype)


def aggregate_blocks(distances, blocks, total):
    count, rows, _ = blocks.shape
    return pl.pallas_call(
        functools.partial(aggregate_kernel, float(total)),
        in_specs=[WHOLE, WHOLE],
        out_specs=[WHOLE, WHOLE],
        out_shape=[
            jax.ShapeDtypeStruct((rows, LANES), blocks.dtype),
            jax.ShapeDtypeStruct((1, LANES), jnp.float32),
        ],
        scratch_shapes=[pltpu.VMEM((count, LANES), jnp.float32)],
        compiler_params=pltpu.CompilerParams(vmem_limit_bytes=32 * MIB),
    )(distances, blocks)


def send(array, first, second):
    pairs = []
    for y in range(SIDE):
        for z in range(SIDE):
            for core in range(CORES):
                dy, dz = (first, second) if core == 0 else (second, first)
                there = (y + dy) % SIDE * SIDE + (z + dz) % SIDE
                pairs.append(((y * SIDE + z) * CORES + core, there * CORES + core))
    return lax.ppermute(array, "rep", pairs)


def swap(array):
    return lax.ppermute(array, "rep", [(i, i ^ 1) for i in range(COUNT)])


def place_kernel(moves, rows, *refs):
    sources, (out, sems) = refs[: len(moves)], refs[-2:]
    me = lax.axis_index("rep")
    y, z, core = me // (SIDE * CORES), me // CORES % SIDE, me % CORES
    stores = []
    for source, pieces in zip(sources, moves):
        for at, first, second, swapped in pieces:
            owner = 1 - core if swapped else core
            dy = jnp.where(owner == 0, first, second)
            dz = jnp.where(owner == 0, second, first)
            block = ((y - dy + SIDE) % SIDE * SIDE + (z - dz + SIDE) % SIDE) * CORES + owner
            target = out.at[pl.ds(pl.multiple_of(block * rows, rows), rows)]
            stores.append(pltpu.make_async_copy(source.at[pl.ds(at, rows)], target, sems.at[len(stores)]))
    for store in stores:
        store.start()
    for store in stores:
        store.wait()


def place(out, rows, sources, moves):
    count = sum(len(m) for m in moves)
    args = list(sources) + ([] if out is None else [out])
    return pl.pallas_call(
        functools.partial(place_kernel, moves, rows),
        in_specs=[WHOLE] * len(sources) + ([] if out is None else [ANY]),
        out_specs=ANY,
        out_shape=jax.ShapeDtypeStruct((COUNT * rows, LANES), sources[0].dtype),
        scratch_shapes=[pltpu.SemaphoreType.DMA((count,))],
        input_output_aliases={} if out is None else {len(args) - 1: 0},
        compiler_params=pltpu.CompilerParams(vmem_limit_bytes=16 * MIB),
        cost_estimate=pl.CostEstimate(flops=0, bytes_accessed=count * rows * LANES * 2, transcendentals=0),
    )(*args)


def after(array, *others):
    return lax.optimization_barrier((array, *others))[0]


def gather(own, *early):
    rows = own.shape[0]

    def moves(firsts, second, swapped):
        return [(k * rows, first, second, swapped) for k, first in enumerate(firsts)]

    up, low = (0, 1), (3, 2)
    one, three, two = send(own, 1, 0), send(own, 3, 0), send(own, 2, 0)
    upper = jnp.concatenate([own, one])
    lower = jnp.concatenate([three, two])
    upper_1, upper_3 = send(upper, 0, 1), send(upper, 0, 3)
    lower_1, lower_3 = send(lower, 0, 1), send(lower, 0, 3)
    upper_2, lower_2 = send(upper_3, 0, 3), send(lower_1, 0, 1)
    out = place(
        None,
        rows,
        [upper, lower, swap(upper), swap(lower)],
        [moves(up, 0, False), moves(low, 0, False), moves(up, 0, True), moves(low, 0, True)],
    )
    swapped = [swap(a) for a in (upper_1, upper_3, after(lower_1, out, *early), after(lower_3, out))]
    layout = [(up, 1), (up, 3), (low, 1), (low, 3)]
    out = place(out, rows, [upper_1, upper_3, lower_1, lower_3], [moves(f, s, False) for f, s in layout])
    far = [swap(after(upper_2, out)), swap(after(lower_2, out))]
    out = place(
        out,
        rows,
        swapped + [upper_2, lower_2],
        [moves(f, s, True) for f, s in layout] + [moves(up, 2, False), moves(low, 2, False)],
    )
    return place(out, rows, far, [moves(up, 2, True), moves(low, 2, True)])


def body(grads):
    count = lax.axis_size("rep")
    total = grads.shape[1] * lax.axis_size("shard")
    slab = compact(grads, 8).reshape(count, -1, LANES)
    blocks = lax.all_to_all(slab, "rep", split_axis=0, concat_axis=0, tiled=True)
    part = partial_distances(blocks, 1)
    everyone = count * lax.axis_size("shard")
    distances = lax.all_to_all(
        jnp.broadcast_to(part[None], (everyone, SHORT, LANES)), ("rep", "shard"), 0, 0, tiled=True
    )
    local, weights = aggregate_blocks(distances, blocks, total)
    weights = weights[0, :count]
    return (gather(local, weights).reshape(-1), weights)


def solution(mesh):
    placed = (P("rep", "shard"),)
    return jax.shard_map(
        body, mesh=mesh, in_specs=placed, out_specs=(P("shard"), P()), check_vma=False
    )
```

```python
import functools

import jax
import jax.numpy as jnp
from jax import lax
from jax.experimental import pallas as pl
from jax.experimental.pallas import tpu as pltpu
from jax.sharding import PartitionSpec as P

ITERS = 4
LANES = 128
PACK = 16
SIDE = 4
CORES = 2
COUNT = SIDE * SIDE * CORES
SHORT = 4
MIB = 1024 * 1024
ANY = pl.BlockSpec(memory_space=pl.ANY)
WHOLE = pl.BlockSpec(memory_space=pltpu.VMEM)


def compact_kernel(parts, piece, x_ref, o_ref, wide, sems):
    size = x_ref.shape[1] // parts
    rows = size // LANES
    loads = [
        pltpu.make_async_copy(x_ref.at[:, pl.ds(i * size, size)], wide.at[:, pl.ds(i * size, size)], sems.at[i])
        for i in range(parts)
    ]
    for load in loads:
        load.start()
    for i in range(parts):
        loads[i].wait()

        @pl.loop(0, rows // piece)
        def _(j):
            at = pl.multiple_of(i * rows + j * piece, piece)
            values = wide[:, pl.ds(pl.multiple_of(at * LANES, piece * LANES), piece * LANES)]
            o_ref[pl.ds(at, piece), :] = values.reshape(piece, LANES)


def compact(grads, parts):
    size = grads.shape[1]
    rows = size // LANES
    return pl.pallas_call(
        functools.partial(compact_kernel, parts, 512),
        in_specs=[ANY],
        out_specs=WHOLE,
        out_shape=jax.ShapeDtypeStruct((rows, LANES), grads.dtype),
        scratch_shapes=[pltpu.VMEM((1, size), grads.dtype), pltpu.SemaphoreType.DMA((parts,))],
        compiler_params=pltpu.CompilerParams(vmem_limit_bytes=40 * MIB),
        cost_estimate=pl.CostEstimate(flops=0, bytes_accessed=6 * size, transcendentals=0),
    )(grads)


def fold(totals):
    wide = totals[0].shape[0]
    i = lax.broadcasted_iota(jnp.int32, (wide, wide), 0)
    j = lax.broadcasted_iota(jnp.int32, (wide, wide), 1)
    same = i % PACK == j % PACK
    groups = wide // PACK
    rows = [jnp.where(same, total, 0.0).reshape(groups, PACK, wide).sum(axis=1) for total in totals]
    k = lax.broadcasted_iota(jnp.int32, (wide, LANES), 0)
    s = lax.broadcasted_iota(jnp.int32, (wide, LANES), 1)
    pick = jnp.where(k // PACK == s, 1.0, 0.0)
    folded = jnp.dot(
        jnp.concatenate(rows, axis=0), pick, precision=lax.Precision.HIGHEST, preferred_element_type=jnp.float32
    )
    return [folded[n * groups : (n + 1) * groups] for n in range(len(totals))]


def grid_of(rows):
    row = lax.broadcasted_iota(jnp.int32, (rows, LANES), 0)
    return row, lax.broadcasted_iota(jnp.int32, (rows, LANES), 1)


def distance_kernel(parts, x_ref, o_ref):
    count, rows, _ = x_ref.shape
    half = count // 2
    rows = rows // parts
    product = functools.partial(
        lax.dot_general, dimension_numbers=(((1,), (1,)), ((), ())), preferred_element_type=jnp.float32
    )

    def group(first, part):
        return jnp.concatenate(
            [
                x_ref[first : first + half, part * rows + j * PACK : part * rows + (j + 1) * PACK, :].reshape(
                    half * PACK, LANES
                )
                for j in range(rows // PACK)
            ],
            axis=1,
        )

    totals = None
    for part in range(parts):
        low, high = group(0, part), group(half, part)
        found = (product(low, low), product(high, low), product(high, high))
        totals = found if totals is None else tuple(a + b for a, b in zip(totals, found))
    low_low, high_low, high_high = fold(totals)
    i, s = grid_of(half)

    def squares(gram):
        own = jnp.where(i == s, gram, 0.0)
        return jnp.sum(own, axis=1, keepdims=True), jnp.sum(own, axis=0, keepdims=True)

    low_down, low_across = squares(low_low)
    high_down, high_across = squares(high_high)
    cross = high_down + low_across - 2.0 * high_low
    within_low = low_down + low_across - 2.0 * low_low
    within_high = high_down + high_across - 2.0 * high_high
    cross = jnp.where(s < half, cross, 0.0)
    within = jnp.where(s < i, within_low, jnp.where((s > i) & (s < half), within_high, 0.0))
    both = cross + pltpu.roll(within, half, 1)
    packed = both[:SHORT]
    for q in range(1, half // SHORT):
        packed = packed + pltpu.roll(both[SHORT * q : SHORT * (q + 1)], count * q, 1)
    o_ref[...] = packed


def partial_distances(blocks, parts):
    return pl.pallas_call(
        functools.partial(distance_kernel, parts),
        in_specs=[WHOLE],
        out_specs=WHOLE,
        out_shape=jax.ShapeDtypeStruct((SHORT, LANES), jnp.float32),
        compiler_params=pltpu.CompilerParams(vmem_limit_bytes=32 * MIB),
    )(blocks)


def all_distances(packed, count):
    half = count // 2
    i, s = grid_of(half)
    both = jnp.concatenate([packed] * (half // SHORT), axis=0)
    both = jnp.where(s // count == i // SHORT, both, 0.0)
    both = sum(pltpu.roll(both, count * q, 1) for q in range(1, half // SHORT)) + both
    turned = jnp.concatenate([both, jnp.zeros((LANES - half, LANES), jnp.float32)], axis=0).T
    cross, cross_turned = jnp.where(s < half, both, 0.0), turned[:half]
    within = jnp.where(s < half, pltpu.roll(both, LANES - half, 1), 0.0)
    within_turned = turned[half:count]
    low = jnp.where(s < i, within, jnp.where(s > i, within_turned, 0.0))
    high = jnp.where(s > i, within, jnp.where(s < i, within_turned, 0.0))
    return jnp.concatenate(
        [low + pltpu.roll(cross_turned, half, 1), cross + pltpu.roll(high, half, 1)], axis=0
    )


def weiszfeld(distances, total):
    count = distances.shape[0]
    r, t = grid_of(count)
    same = (t == r).astype(jnp.float32)
    weights = jnp.full((count, 1), 1.0 / count, jnp.float32)
    for _ in range(ITERS):
        across = jnp.sum(same * weights, axis=0, keepdims=True)
        query = jnp.sum(distances * across, axis=1, keepdims=True)
        spread = jnp.sum(weights * query, axis=0, keepdims=True)
        square = jnp.maximum((query - 0.5 * spread) / total, 0.0)
        inverse = 1.0 / jnp.sqrt(square + 1e-06)
        weights = inverse / jnp.sum(inverse, axis=0, keepdims=True)
    return weights, jnp.sum(same * weights, axis=0, keepdims=True)


def add_up(ref, ways=8):
    each = ref.shape[0] // ways
    sums = [ref[n * each] for n in range(ways)]
    for k in range(1, each):
        sums = [total + ref[n * each + k] for n, total in enumerate(sums)]
    while len(sums) > 1:
        sums = [a + b for a, b in zip(sums[::2], sums[1::2])]
    return sums[0]


def aggregate_kernel(total, d_ref, x_ref, o_ref, w_ref, coeffs):
    count, rows, _ = x_ref.shape
    weights, across = weiszfeld(all_distances(add_up(d_ref), count), total)
    w_ref[...] = across
    coeffs[...] = jnp.broadcast_to(weights.astype(jnp.bfloat16).astype(jnp.float32), (count, LANES))
    piece = 64

    @pl.loop(0, rows // piece)
    def _(k):
        at = pl.ds(pl.multiple_of(k * piece, piece), piece)
        sums = [None] * 4
        for r in range(count):
            term = x_ref[r, at, :].astype(jnp.float32) * coeffs[r : r + 1, :]
            sums[r % 4] = term if sums[r % 4] is None else sums[r % 4] + term
        o_ref[at, :] = ((sums[0] + sums[1]) + (sums[2] + sums[3])).astype(o_ref.dtype)


def aggregate_blocks(distances, blocks, total):
    count, rows, _ = blocks.shape
    return pl.pallas_call(
        functools.partial(aggregate_kernel, float(total)),
        in_specs=[WHOLE, WHOLE],
        out_specs=[WHOLE, WHOLE],
        out_shape=[
            jax.ShapeDtypeStruct((rows, LANES), blocks.dtype),
            jax.ShapeDtypeStruct((1, LANES), jnp.float32),
        ],
        scratch_shapes=[pltpu.VMEM((count, LANES), jnp.float32)],
        compiler_params=pltpu.CompilerParams(vmem_limit_bytes=32 * MIB),
    )(distances, blocks)


def send(array, first, second):
    pairs = []
    for y in range(SIDE):
        for z in range(SIDE):
            for core in range(CORES):
                dy, dz = (first, second) if core == 0 else (second, first)
                there = (y + dy) % SIDE * SIDE + (z + dz) % SIDE
                pairs.append(((y * SIDE + z) * CORES + core, there * CORES + core))
    return lax.ppermute(array, "rep", pairs)


def swap(array):
    return lax.ppermute(array, "rep", [(i, i ^ 1) for i in range(COUNT)])


def place_kernel(moves, rows, *refs):
    sources, (out, sems) = refs[: len(moves)], refs[-2:]
    me = lax.axis_index("rep")
    y, z, core = me // (SIDE * CORES), me // CORES % SIDE, me % CORES
    stores = []
    for source, pieces in zip(sources, moves):
        for at, first, second, swapped in pieces:
            owner = 1 - core if swapped else core
            dy = jnp.where(owner == 0, first, second)
            dz = jnp.where(owner == 0, second, first)
            block = ((y - dy + SIDE) % SIDE * SIDE + (z - dz + SIDE) % SIDE) * CORES + owner
            target = out.at[pl.ds(pl.multiple_of(block * rows, rows), rows)]
            stores.append(pltpu.make_async_copy(source.at[pl.ds(at, rows)], target, sems.at[len(stores)]))
    for store in stores:
        store.start()
    for store in stores:
        store.wait()


def place(out, rows, sources, moves):
    count = sum(len(m) for m in moves)
    args = list(sources) + ([] if out is None else [out])
    return pl.pallas_call(
        functools.partial(place_kernel, moves, rows),
        in_specs=[WHOLE] * len(sources) + ([] if out is None else [ANY]),
        out_specs=ANY,
        out_shape=jax.ShapeDtypeStruct((COUNT * rows, LANES), sources[0].dtype),
        scratch_shapes=[pltpu.SemaphoreType.DMA((count,))],
        input_output_aliases={} if out is None else {len(args) - 1: 0},
        compiler_params=pltpu.CompilerParams(vmem_limit_bytes=16 * MIB),
        cost_estimate=pl.CostEstimate(flops=0, bytes_accessed=count * rows * LANES * 2, transcendentals=0),
    )(*args)


def after(array, *others):
    return lax.optimization_barrier((array, *others))[0]


def gather(own, *early):
    rows = own.shape[0]

    def moves(firsts, second, swapped):
        return [(k * rows, first, second, swapped) for k, first in enumerate(firsts)]

    up, low = (0, 1), (3, 2)
    one, three, two = send(own, 1, 0), send(own, 3, 0), send(own, 2, 0)
    upper = jnp.concatenate([own, one])
    lower = jnp.concatenate([three, two])
    upper_1, upper_3 = send(upper, 0, 1), send(upper, 0, 3)
    lower_1, lower_3 = send(lower, 0, 1), send(lower, 0, 3)
    upper_2, lower_2 = send(upper_3, 0, 3), send(lower_1, 0, 1)
    out = place(
        None,
        rows,
        [upper, lower, swap(upper), swap(lower)],
        [moves(up, 0, False), moves(low, 0, False), moves(up, 0, True), moves(low, 0, True)],
    )
    swapped = [swap(a) for a in (upper_1, upper_3, after(lower_1, out, *early), after(lower_3, out))]
    layout = [(up, 1), (up, 3), (low, 1), (low, 3)]
    out = place(out, rows, [upper_1, upper_3, lower_1, lower_3], [moves(f, s, False) for f, s in layout])
    far = [swap(after(upper_2, out)), swap(after(lower_2, out))]
    out = place(
        out,
        rows,
        swapped + [upper_2, lower_2],
        [moves(f, s, True) for f, s in layout] + [moves(up, 2, False), moves(low, 2, False)],
    )
    return place(out, rows, far, [moves(up, 2, True), moves(low, 2, True)])


def body(grads):
    count = lax.axis_size("rep")
    total = grads.shape[1] * lax.axis_size("shard")
    slab = compact(grads, 16).reshape(count, -1, LANES)
    blocks = lax.all_to_all(slab, "rep", split_axis=0, concat_axis=0, tiled=True)
    part = partial_distances(blocks, 1)
    everyone = count * lax.axis_size("shard")
    distances = lax.all_to_all(
        jnp.broadcast_to(part[None], (everyone, SHORT, LANES)), ("rep", "shard"), 0, 0, tiled=True
    )
    local, weights = aggregate_blocks(distances, blocks, total)
    weights = weights[0, :count]
    return (gather(local, weights).reshape(-1), weights)


def solution(mesh):
    placed = (P("rep", "shard"),)
    return jax.shard_map(
        body, mesh=mesh, in_specs=placed, out_specs=(P("shard"), P()), check_vma=False
    )
```
